256 devices in a mesh: layer: 8 (over y, z_lo), lat: 32 (over x, z_hi, core).
Axes of the slice: x: 4, y: 4, z: 8 (z_hi: 4, z_lo: 2; z = z_hi * 2 + z_lo), core: 2. Of those that a mesh axis runs over, the one named last changes fastest.
Arguments:
- acts: bfloat16 [8, 512, 2304], P('layer', 'lat'), may hold values from -6 to 6
- enc_weight: bfloat16 [8, 2304, 40960], P('layer', None, 'lat'), may hold values from -0.046875 to 0.046875
- enc_scale: float32 [8, 18, 320], P('layer', None, 'lat'), may hold values from 0.5 to 2
- enc_bias: float32 [40960], P('lat'), may hold values from -3 to 3
- dec_weight: bfloat16 [8, 40960, 2304], P('layer', 'lat'), may hold values from -0.03125 to 0.03125
- dec_scale: float32 [8, 320, 18], P('layer', 'lat'), may hold values from 0.5 to 2
- dec_bias: float32 [8, 2304], P('layer'), may hold values from -3 to 3
Outputs:
- recon: bfloat16 [8, 512, 2304], P('layer', 'lat')
- latents: bfloat16 [512, 40960], P(None, 'lat')
The draws below stay inside these ranges and needn't reach their ends.
All inputs are finite; a program needn't handle non-finite values.
Results may differ from the reference program's by a relative error of at most 0.025.
Values may be sent and summed in bfloat16 or wider, within the bound.
No kernel may reach another device: no remote copies, remote signals or barrier semaphores. Data moves between devices by JAX's collectives and lax.ppermute only.
A program may use at most 64 MiB of HBM per device.

```python
import math
import jax
import jax.numpy as jnp
from jax import lax

D = 2304
LAT_DEV = 1280
BLOCK = 128
LAYERS = 8
LAT = 40960
TOKENS = 512
N_LAT = 32


def block_scale(key, shape, pieces, low, top_value):
    gain, own = 1.0, jax.random.fold_in(key, 6)
    for position, shards_of in pieces:
        heights = jnp.exp(jax.random.uniform(jax.random.fold_in(own, position), (shards_of,), jnp.float32, low / len(pieces), top_value / len(pieces)))
        gain = gain * jnp.repeat(heights, shape[position] // shards_of).reshape([-1 if axis == position else 1 for axis in range(len(shape))])
    return gain


def centred(key, dims, width, bound, pieces=(), held_as=jnp.bfloat16):
    array = jax.random.normal(key, dims, jnp.float32) * width
    if len(pieces) > 0:
        array = block_scale(key, dims, pieces, -0.22, 0.18) * array
    return jnp.clip(array, min=-bound, max=bound).astype(held_as)


def setup_inputs(seed: int = 0) -> dict:
    seeds = jax.random.split(jax.random.key(seed), 8)
    return {
        "acts": centred(seeds[0], (LAYERS, TOKENS, D), 1.0, 6.0, ((0, 8), (1, 32))),
        "enc_weight": centred(seeds[1], (LAYERS, D, LAT), (D * LAYERS) ** -0.5, 0.046875, ((0, 8), (2, 32))),
        "enc_scale": jnp.clip(jnp.exp(math.log(2.0) - 1.3862944 * jax.random.uniform(seeds[2], (LAYERS, D // BLOCK, LAT // BLOCK), jnp.float32) ** block_scale(seeds[2], (LAYERS, D // BLOCK, LAT // BLOCK), ((0, 8), (2, 32)), -0.2, 0.2)), 0.5, 2.0),
        "enc_bias": centred(seeds[3], (LAT,), 0.5, 3.0, ((0, 32),), jnp.float32),
        "dec_weight": centred(seeds[4], (LAYERS, LAT, D), LAT ** -0.5, 0.03125, ((0, 8), (1, 32))),
        "dec_scale": jnp.clip(jnp.exp(math.log(2.0) - 1.3862944 * jax.random.uniform(seeds[5], (LAYERS, LAT // BLOCK, D // BLOCK), jnp.float32) ** block_scale(seeds[5], (LAYERS, LAT // BLOCK, D // BLOCK), ((0, 8), (1, 32)), -0.2, 0.2)), 0.5, 2.0),
        "dec_bias": centred(seeds[6], (LAYERS, D), 0.5, 3.0, ((0, 8),), jnp.float32),
    }


def dequant(quant, scale):
    full = jnp.repeat(jnp.repeat(scale, BLOCK, axis=-2), BLOCK, axis=-1)
    return (quant.astype(jnp.float32) * full).astype(jnp.bfloat16)


def reference(acts, enc_weight, enc_scale, enc_bias, dec_weight, dec_scale, dec_bias):
    def encode(total, items):
        layer_acts, weight, scale = items
        full = dequant(weight, scale)
        return total + jnp.dot(layer_acts, full, preferred_element_type=jnp.float32), None

    start = jnp.zeros((TOKENS, LAT), jnp.float32)
    preact, unused = lax.scan(encode, start, (acts, enc_weight, enc_scale))
    preact = preact + enc_bias[None, :]
    latents = jnp.maximum(preact, 0.0).astype(jnp.bfloat16)
    blocked = latents.reshape(TOKENS, N_LAT, LAT_DEV).astype(jnp.float32)

    def decode(items):
        weight, scale, bias = items
        full = dequant(weight, scale).reshape(N_LAT, LAT_DEV, D).astype(jnp.float32)
        parts = jnp.einsum("tnk,nkd->ntd", blocked, full).astype(jnp.bfloat16)
        parts = lax.optimization_barrier(parts).astype(jnp.float32)
        return (jnp.sum(parts, axis=0) + bias[None, :]).astype(jnp.bfloat16)

    recon = lax.map(decode, (dec_weight, dec_scale, dec_bias))
    return recon, latents
```

```python
import functools

import jax
import jax.numpy as jnp
from jax import lax
from jax.experimental import pallas as pl
from jax.experimental.pallas import tpu as pltpu
from jax.sharding import Mesh, PartitionSpec as P

BLOCK = 128
Y, ZL, X, ZH, C = 4, 2, 4, 4, 2
LAYER, LAT = ("y", "zl"), ("x", "zh", "c")
F32, BF16 = jnp.float32, jnp.bfloat16
MIB = 1 << 20


def params(mib):
    return pltpu.CompilerParams(vmem_limit_bytes=mib * MIB)


def cost(flops, moved):
    return pl.CostEstimate(flops=flops, bytes_accessed=moved, transcendentals=0)


def dequant_kernel(scale_ref, w_ref, out_ref):
    step = pl.program_id(0)
    rows, columns = w_ref.shape
    for i in range(rows // BLOCK):
        for j in range(columns // BLOCK):
            at = (slice(i * BLOCK, (i + 1) * BLOCK), slice(j * BLOCK, (j + 1) * BLOCK))
            scale = scale_ref[step * (rows // BLOCK) + i, j]
            out_ref[at] = (w_ref[at].astype(F32) * scale).astype(BF16)


def dequant(weight, scale):
    depth, width = weight.shape
    rows = 2 * BLOCK
    return pl.pallas_call(
        dequant_kernel,
        grid=(depth // rows,),
        in_specs=[
            pl.BlockSpec(memory_space=pltpu.SMEM),
            pl.BlockSpec((rows, width), lambda i: (i, 0)),
        ],
        out_specs=pl.BlockSpec((rows, width), lambda i: (i, 0)),
        out_shape=jax.ShapeDtypeStruct((depth, width), BF16),
        compiler_params=params(16),
        cost_estimate=cost(depth * width, 4 * depth * width),
        name="dequant",
    )(scale, weight)


def encode_kernel(*refs):
    pieces, w_ref, out_ref, rows_ref = refs[:-3], refs[-3], refs[-2], refs[-1]
    height = pieces[0].shape[0]

    @pl.when(pl.program_id(0) == 0)
    def _():
        for k, piece in enumerate(pieces):
            rows_ref[k * height : (k + 1) * height, :] = piece[...]

    out_ref[...] = jnp.dot(rows_ref[...], w_ref[...], preferred_element_type=F32).astype(BF16)


def encode(pieces, weight):
    depth, width = weight.shape
    height = pieces[0].shape[0]
    total, tile = height * len(pieces), 256
    return pl.pallas_call(
        encode_kernel,
        grid=(width // tile,),
        in_specs=[pl.BlockSpec((height, depth), lambda i: (0, 0))] * len(pieces)
        + [pl.BlockSpec((depth, tile), lambda i: (0, i))],
        out_specs=pl.BlockSpec((total, tile), lambda i: (0, i)),
        out_shape=jax.ShapeDtypeStruct((total, width), BF16),
        scratch_shapes=[pltpu.VMEM((total, depth), BF16)],
        compiler_params=params(16),
        cost_estimate=cost(2 * total * depth * width, 2 * (depth * width + total * (depth + width))),
        name="encode",
    )(*pieces, weight)


def activate_kernel(terms_ref, bias_ref, out_ref):
    preact = jnp.sum(terms_ref[...].astype(F32), axis=0) + bias_ref[...]
    latents = jnp.maximum(preact, 0.0).astype(BF16)
    for m in range(out_ref.shape[0]):
        out_ref[m] = latents


def activate(terms, bias):
    members, height, width = terms.shape
    tile = 256
    return pl.pallas_call(
        activate_kernel,
        grid=(width // tile,),
        in_specs=[
            pl.BlockSpec((members, height, tile), lambda i: (0, 0, i)),
            pl.BlockSpec((1, tile), lambda i: (0, i)),
        ],
        out_specs=pl.BlockSpec((members, height, tile), lambda i: (0, 0, i)),
        out_shape=jax.ShapeDtypeStruct(terms.shape, BF16),
        compiler_params=params(16),
        cost_estimate=cost(terms.size, 4 * terms.size),
        name="activate",
    )(terms, bias)


def place_kernel(where_ref, latents_ref, out_ref, sem):
    x, zh, c = where_ref[0], where_ref[1], where_ref[2]
    height = 16
    copies = []
    for kc in range(C):
        for kx in range(X):
            for kz in range(ZH):
                b = (kc * X + kx) * ZH + kz
                owner = (((x + kx) % X) * ZH + (zh + kz) % ZH) * C + (c + kc) % C
                copies.append(
                    pltpu.make_async_copy(
                        latents_ref.at[pl.ds(b * height, height), :],
                        out_ref.at[pl.ds(pl.multiple_of(owner * height, height), height), :],
                        sem.at[b],
                    )
                )
    for copy in copies:
        copy.start()
    for copy in copies:
        copy.wait()


def place(where, latents):
    return pl.pallas_call(
        place_kernel,
        in_specs=[pl.BlockSpec(memory_space=pltpu.SMEM), pl.BlockSpec(memory_space=pl.ANY)],
        out_specs=pl.BlockSpec(memory_space=pl.ANY),
        out_shape=jax.ShapeDtypeStruct(latents.shape, BF16),
        scratch_shapes=[pltpu.SemaphoreType.DMA((C * X * ZH,))],
        compiler_params=params(4),
        cost_estimate=cost(0, 4 * latents.size),
        name="place",
    )(where, latents)


def decode_kernel(latents_ref, w_ref, out_ref):
    out_ref[...] = jnp.dot(latents_ref[...], w_ref[...], preferred_element_type=F32).astype(BF16)


def decode(latents, weight, half):
    depth, width = weight.shape
    total, tile = latents.shape[0] // 2, 256
    return pl.pallas_call(
        decode_kernel,
        grid=(width // tile,),
        in_specs=[
            pl.BlockSpec((total, depth), lambda i: (half, 0)),
            pl.BlockSpec((depth, tile), lambda i: (0, i)),
        ],
        out_specs=pl.BlockSpec((total, tile), lambda i: (0, i)),
        out_shape=jax.ShapeDtypeStruct((total, width), BF16),
        compiler_params=params(16),
        cost_estimate=cost(2 * total * depth * width, 2 * (depth * width + total * (depth + width))),
        name="decode",
    )(latents, weight)


def total_kernel(*refs, terms, bias):
    ins, outs = refs[: terms + bias], refs[terms + bias :]
    total = ins[0][...].astype(F32)
    for ref in ins[1:]:
        total = total + ref[...].astype(F32)
    height = outs[0].shape[0]
    for k, out in enumerate(outs):
        out[...] = total[k * height : (k + 1) * height].astype(BF16)


def total(arrays, cuts, bias=None):
    height, width = arrays[0].shape
    ins = list(arrays) + ([] if bias is None else [bias])
    out = jax.ShapeDtypeStruct((height // cuts, width), BF16)
    return pl.pallas_call(
        functools.partial(total_kernel, terms=len(arrays), bias=bias is not None),
        in_specs=[pl.BlockSpec(memory_space=pltpu.VMEM)] * len(ins),
        out_specs=[pl.BlockSpec(memory_space=pltpu.VMEM)] * cuts,
        out_shape=[out] * cuts,
        compiler_params=params(24),
        cost_estimate=cost(height * width, 2 * (len(arrays) + 1) * height * width),
        name="total",
    )(*ins)


def send(array, axis, size, by):
    return lax.ppermute(array, axis, [(i, (i + by) % size) for i in range(size)])


def on_device(acts, enc_weight, enc_scale, enc_bias, dec_weight, dec_scale, dec_bias):
    where = jnp.stack([lax.axis_index("x"), lax.axis_index("zh"), lax.axis_index("c")]).astype(jnp.int32)
    own = acts[0]
    column = jnp.concatenate([own] + [send(own, "zh", ZH, -k) for k in (1, 2, 3)], axis=0)
    mine = [column] + [send(column, "x", X, -k) for k in (1, 2, 3)]
    other = [send(piece, "c", C, 1) for piece in mine]
    enc_full = dequant(enc_weight[0], enc_scale[0])
    dec_full = dequant(dec_weight[0], dec_scale[0])
    terms = jnp.concatenate([encode(mine, enc_full), encode(other, enc_full)], axis=0)
    members = Y * ZL
    terms = terms.reshape(members, terms.shape[0] // members, terms.shape[1])
    terms = lax.all_to_all(terms, LAYER, 0, 0, tiled=True)
    copies = activate(terms, enc_bias[None, :])
    latents = lax.all_to_all(copies, LAYER, 0, 0, tiled=True)
    latents = latents.reshape(-1, latents.shape[-1])
    theirs = send(decode(latents, dec_full, 1), "c", C, 1)
    part = total([decode(latents, dec_full, 0), theirs], X)
    part = total([part[0]] + [send(part[k], "x", X, k) for k in (1, 2, 3)], ZH)
    recon = total([part[0]] + [send(part[k], "zh", ZH, k) for k in (1, 2, 3)], 1, dec_bias)[0]
    return (recon[None], place(where, latents))


def solution(mesh):
    axes = ("y", "zl", "x", "zh", "c")
    fine = Mesh(mesh.devices.reshape(Y, ZL, X, ZH, C), axes)
    in_specs = (
        P(LAYER, LAT, None),
        P(LAYER, None, LAT),
        P(LAYER, None, LAT),
        P(LAT),
        P(LAYER, LAT, None),
        P(LAYER, LAT, None),
        P(LAYER, None),
    )
    out_specs = (P(LAYER, LAT, None), P(None, LAT))
    return jax.shard_map(on_device, mesh=fine, in_specs=in_specs, out_specs=out_specs, check_vma=False)
```

```python
import functools

import jax
import jax.numpy as jnp
from jax import lax
from jax.experimental import pallas as pl
from jax.experimental.pallas import tpu as pltpu
from jax.sharding import Mesh, PartitionSpec as P

BLOCK = 128
Y, ZL, X, ZH, C = 4, 2, 4, 4, 2
LAYER, LAT = ("y", "zl"), ("x", "zh", "c")
AROUND = (1, 3, 2)
F32, BF16 = jnp.float32, jnp.bfloat16
MIB = 1 << 20
IN_VMEM = pl.BlockSpec(memory_space=pltpu.VMEM)
IN_SMEM = pl.BlockSpec(memory_space=pltpu.SMEM)
ANYWHERE = pl.BlockSpec(memory_space=pl.ANY)


def params(mib):
    return pltpu.CompilerParams(vmem_limit_bytes=mib * MIB)


def cost(flops, moved):
    return pl.CostEstimate(flops=flops, bytes_accessed=moved, transcendentals=0)


def shape(*dims):
    return jax.ShapeDtypeStruct(dims, BF16)


def whole(kernel, ins, outs, name, flops=0, mib=16, where=None):
    moved = sum(a.size * a.dtype.itemsize for a in list(ins) + list(outs))
    place = [] if where is None else [where]
    return pl.pallas_call(
        kernel,
        in_specs=[IN_SMEM] * len(place) + [IN_VMEM] * len(ins),
        out_specs=[IN_VMEM] * len(outs),
        out_shape=list(outs),
        compiler_params=params(mib),
        cost_estimate=cost(flops, moved),
        name=name,
    )(*place, *ins)


def dequant_kernel(scale_ref, w_ref, out_ref, raw_ref, sem, *, by_row):
    rows, width = out_ref.shape
    step, steps = pl.program_id(0), raw_ref.shape[0] // rows

    def read(step):
        at = pl.ds(pl.multiple_of(step * rows, rows), rows)
        return pltpu.make_async_copy(w_ref.at[at, :], raw_ref.at[at, :], sem.at[step])

    @pl.when(step == 0)
    def _():
        for k in range(steps):
            read(k).start()

    read(step).wait()
    for i in range(rows // BLOCK):
        at = pl.ds(pl.multiple_of(step * rows + i * BLOCK, BLOCK), BLOCK)
        for j in range(width // BLOCK):
            columns = slice(j * BLOCK, (j + 1) * BLOCK)
            k = step * (rows // BLOCK) + i
            scale = scale_ref[k, 0, j] if by_row else scale_ref[j, 0, k]
            out_ref[i * BLOCK : (i + 1) * BLOCK, columns] = (raw_ref[at, columns].astype(F32) * scale).astype(BF16)


def dequant(weight, scale, rows, by_row):
    depth, width = weight.shape
    return pl.pallas_call(
        functools.partial(dequant_kernel, by_row=by_row),
        grid=(depth // rows,),
        in_specs=[IN_SMEM, ANYWHERE],
        out_specs=pl.BlockSpec((rows, width), lambda i: (i, 0)),
        out_shape=shape(depth, width),
        scratch_shapes=[pltpu.VMEM((depth, width), BF16), pltpu.SemaphoreType.DMA((depth // rows,))],
        compiler_params=params(16),
        cost_estimate=cost(depth * width, 4 * depth * width),
        name="dequant",
    )(scale, pltpu.with_memory_space_constraint(weight, pltpu.HBM))


def product(rows, w_ref, store, width=256):
    for j in range(w_ref.shape[1] // width):
        at = slice(j * width, (j + 1) * width)
        store(at, jnp.dot(rows, w_ref[:, at], preferred_element_type=F32).astype(BF16))


def encode_kernel(where_ref, mine_ref, theirs_ref, w_ref, *refs):
    outs, all_ref = refs[:Y], refs[Y]
    height = outs[0].shape[0]
    y = where_ref[0]
    rows = jnp.concatenate([mine_ref[...], theirs_ref[...]], axis=0)

    def store(at, tile):
        all_ref[:, at] = tile

    product(rows, w_ref, store)
    for r, out in enumerate(outs):
        quarter = lax.rem(y + r, Y)
        out[...] = all_ref[pl.ds(pl.multiple_of(quarter * height, height), height), :]


def encode(where, mine, theirs, weight):
    depth, width = weight.shape
    rows = mine.shape[0] + theirs.shape[0]
    return pl.pallas_call(
        encode_kernel,
        in_specs=[IN_SMEM] + [IN_VMEM] * 3,
        out_specs=[IN_VMEM] * Y,
        out_shape=[shape(rows // Y, width)] * Y,
        scratch_shapes=[pltpu.VMEM((rows, width), BF16)],
        compiler_params=params(16),
        cost_estimate=cost(2 * rows * depth * width, 2 * depth * width),
        name="encode",
    )(where, mine, theirs, weight)


def decode_kernel(where_ref, *refs):
    quarters, w_ref, mine_ref, theirs_ref, all_ref = refs[:Y], refs[Y], refs[Y + 1], refs[Y + 2], refs[Y + 3]
    height, half = quarters[0].shape[0], mine_ref.shape[0]
    y = where_ref[0]
    for r, ref in enumerate(quarters):
        quarter = lax.rem(y + r, Y)
        all_ref[pl.ds(pl.multiple_of(quarter * height, height), height), :] = ref[...]

    def store(at, tile):
        mine_ref[:, at] = tile[:half]
        theirs_ref[:, at] = tile[half:]

    product(all_ref[...], w_ref, store)


def decode(where, quarters, weight):
    depth, width = weight.shape
    rows = quarters[0].shape[0] * Y
    return pl.pallas_call(
        decode_kernel,
        in_specs=[IN_SMEM] + [IN_VMEM] * (Y + 1),
        out_specs=[IN_VMEM] * 2,
        out_shape=[shape(rows // 2, width)] * 2,
        scratch_shapes=[pltpu.VMEM((rows, depth), BF16)],
        compiler_params=params(16),
        cost_estimate=cost(2 * rows * depth * width, 2 * depth * width),
        name="decode",
    )(where, *quarters, weight)


def join_kernel(*refs):
    height = refs[0].shape[0]
    for k, ref in enumerate(refs[:-1]):
        refs[-1][k * height : (k + 1) * height, :] = ref[...]


def sum_kernel(*refs, terms):
    ins, outs = refs[:terms], refs[terms:]
    height = outs[0].shape[0]
    for k, out in enumerate(outs):
        at = slice(k * height, (k + 1) * height)
        total = ins[0][at, :].astype(F32)
        for ref in ins[1:]:
            total = total + ref[at, :].astype(F32)
        out[...] = total.astype(BF16)


def added(arrays, cuts, name):
    rows, width = arrays[0].shape
    return whole(
        functools.partial(sum_kernel, terms=len(arrays)), arrays, [shape(rows // cuts, width)] * cuts, name
    )


def activate_kernel(a_ref, b_ref, bias_ref, out_ref):
    preact = (a_ref[...].astype(F32) + b_ref[...].astype(F32)) + bias_ref[...].reshape(1, -1)
    out_ref[...] = jnp.maximum(preact, 0.0).astype(BF16)


def finish_kernel(*refs):
    total = refs[-2][...]
    for ref in refs[:-2]:
        total = total + ref[...].astype(F32)
    refs[-1][...] = total.astype(BF16)


def place_kernel(where_ref, *refs):
    latents, out_ref, sem = refs[:-2], refs[-2], refs[-1]
    y, x, zh, c = (where_ref[i] for i in range(4))
    height = 16
    blocks = latents[0].shape[0] // height
    copies = []
    for a, ref in enumerate(latents):
        n, quarter = a // Y, lax.rem(y + a % Y, Y)
        for j in range(blocks):
            b = quarter * blocks + j
            kc, kx, k = b // (2 * X), lax.rem(b // 2, X), lax.rem(b, 2)
            owner = (lax.rem(x + kx, X) * ZH + lax.rem(zh + 2 * (1 - n) + k, ZH)) * C + lax.rem(c + kc, C)
            copies.append(
                pltpu.make_async_copy(
                    ref.at[pl.ds(j * height, height), :],
                    out_ref.at[pl.ds(pl.multiple_of(owner * height, height), height), :],
                    sem.at[a * blocks + j],
                )
            )
    for copy in copies:
        copy.start()
    for copy in copies:
        copy.wait()


def place(where, latents):
    rows, width = latents[0].shape
    rows *= len(latents)
    return pl.pallas_call(
        place_kernel,
        in_specs=[IN_SMEM] + [ANYWHERE] * len(latents),
        out_specs=ANYWHERE,
        out_shape=shape(rows, width),
        scratch_shapes=[pltpu.SemaphoreType.DMA((rows // 16,))],
        compiler_params=params(4),
        cost_estimate=cost(0, 4 * rows * width),
        name="place",
    )(where, *latents)


def after(array, *others):
    return lax.optimization_barrier((array,) + others)[0]


def send(array, axis, size, by):
    return lax.ppermute(array, axis, [(i, (i + by) % size) for i in range(size)])


def fetch_around(array, axis, size):
    got = {k: send(array, axis, size, -k) for k in AROUND}
    return [array] + [got[k] for k in (1, 2, 3)]


def hand_around(arrays, axis, size):
    return [arrays[0]] + [send(arrays[k], axis, size, k) for k in AROUND]


def on_device(acts, enc_weight, enc_scale, enc_bias, dec_weight, dec_scale, dec_bias):
    depth, width = enc_weight.shape[1:]
    own = acts[0]
    rows = own.shape[0]
    chunk = 2 * rows
    where = jnp.stack([lax.axis_index(a) for a in ("y", "x", "zh", "c")]).astype(jnp.int32)
    near, far, back = (send(own, "zh", ZH, -k) for k in (1, 2, 3))
    enc_full = dequant(enc_weight[0], after(jnp.transpose(enc_scale, (2, 0, 1)), where), 2 * BLOCK, False)
    pairs = ([far, after(back, enc_full, near)], [own, near])
    quarters, pieces, terms = [], None, None
    for n, pair in enumerate(pairs):
        if n == 1:
            pair[1] = after(pair[1], pieces[1])
        column = whole(join_kernel, pair, [shape(chunk, depth)], "join")[0]
        pieces = fetch_around(column, "x", X)
        if n == 1:
            pieces[1] = after(pieces[1], terms[0])
        mine = whole(join_kernel, pieces, [shape(X * chunk, depth)], "join")[0]
        theirs = send(mine, "c", C, 1)
        terms = list(encode(where, mine, theirs, enc_full))
        if n == 0:
            dec_full = dequant(dec_weight[0], after(jnp.transpose(dec_scale, (1, 0, 2)), terms[0]), BLOCK, True)
            terms[0] = after(terms[0], dec_full)
        part = added(hand_around(terms, "y", Y), 1, "gather")[0]
        latents = whole(activate_kernel, [part, send(part, "zl", ZL, 1), enc_bias], [shape(*part.shape)], "activate")[0]
        quarters.append(fetch_around(latents, "y", Y))
    parts, done = [], None
    for n in range(2):
        latents = list(quarters[n])
        if done is not None:
            latents[0] = after(latents[0], done)
        mine, theirs = decode(where, latents, dec_full)
        done = mine
        cuts = added([mine, send(theirs, "c", C, 1)], X, "add")
        low, high = added(hand_around(cuts, "x", X), 2, "fold")
        parts += [send(low, "zh", ZH, 2), send(high, "zh", ZH, 3)] if n == 0 else [low, send(high, "zh", ZH, 1)]
    recon = whole(finish_kernel, parts + [dec_bias], [shape(rows, depth)], "finish")[0]
    return (recon[None], place(where, quarters[0] + quarters[1]))


def solution(mesh):
    axes = ("y", "zl", "x", "zh", "c")
    fine = Mesh(mesh.devices.reshape(Y, ZL, X, ZH, C), axes)
    in_specs = (
        P(LAYER, LAT, None),
        P(LAYER, None, LAT),
        P(LAYER, None, LAT),
        P(LAT),
        P(LAYER, LAT, None),
        P(LAYER, LAT, None),
        P(LAYER, None),
    )
    out_specs = (P(LAYER, LAT, None), P(None, LAT))
    return jax.shard_map(on_device, mesh=fine, in_specs=in_specs, out_specs=out_specs, check_vma=False)
```

```python
import functools

import jax
import jax.numpy as jnp
from jax import lax
from jax.experimental import pallas as pl
from jax.experimental.pallas import tpu as pltpu
from jax.sharding import Mesh, PartitionSpec as P

BLOCK = 128
Y, ZL, X, ZH, C = 4, 2, 4, 4, 2
LAYER, LAT = ("y", "zl"), ("x", "zh", "c")
ORDER = (0, 2, 1, 3)
SENT = (2, 3, 1)
F32, BF16 = jnp.float32, jnp.bfloat16
MIB = 1 << 20
IN_VMEM = pl.BlockSpec(memory_space=pltpu.VMEM)
IN_SMEM = pl.BlockSpec(memory_space=pltpu.SMEM)
ANYWHERE = pl.BlockSpec(memory_space=pl.ANY)


def params(mib):
    return pltpu.CompilerParams(vmem_limit_bytes=mib * MIB)


def cost(flops, moved):
    return pl.CostEstimate(flops=flops, bytes_accessed=moved, transcendentals=0)


def shape(*dims):
    return jax.ShapeDtypeStruct(dims, BF16)


def whole(kernel, ins, outs, name, flops=0, mib=16, where=None):
    moved = sum(a.size * a.dtype.itemsize for a in list(ins) + list(outs))
    place = [] if where is None else [where]
    return pl.pallas_call(
        kernel,
        in_specs=[IN_SMEM] * len(place) + [IN_VMEM] * len(ins),
        out_specs=[IN_VMEM] * len(outs),
        out_shape=list(outs),
        compiler_params=params(mib),
        cost_estimate=cost(flops, moved),
        name=name,
    )(*place, *ins)


def dequant_kernel(scale_ref, w_ref, out_ref, raw_ref, sem, *, by_row):
    rows, width = out_ref.shape
    step, steps = pl.program_id(0), raw_ref.shape[0] // rows

    def read(step):
        at = pl.ds(pl.multiple_of(step * rows, rows), rows)
        return pltpu.make_async_copy(w_ref.at[at, :], raw_ref.at[at, :], sem.at[step])

    @pl.when(step == 0)
    def _():
        for k in range(steps):
            read(k).start()

    read(step).wait()
    for i in range(rows // BLOCK):
        at = pl.ds(pl.multiple_of(step * rows + i * BLOCK, BLOCK), BLOCK)
        for j in range(width // BLOCK):
            columns = slice(j * BLOCK, (j + 1) * BLOCK)
            k = step * (rows // BLOCK) + i
            scale = scale_ref[k, 0, j] if by_row else scale_ref[j, 0, k]
            out_ref[i * BLOCK : (i + 1) * BLOCK, columns] = (raw_ref[at, columns].astype(F32) * scale).astype(BF16)


def dequant(weight, scale, rows, by_row):
    depth, width = weight.shape
    return pl.pallas_call(
        functools.partial(dequant_kernel, by_row=by_row),
        grid=(depth // rows,),
        in_specs=[IN_SMEM, ANYWHERE],
        out_specs=pl.BlockSpec((rows, width), lambda i: (i, 0)),
        out_shape=shape(depth, width),
        scratch_shapes=[pltpu.VMEM((depth, width), BF16), pltpu.SemaphoreType.DMA((depth // rows,))],
        compiler_params=params(16),
        cost_estimate=cost(depth * width, 4 * depth * width),
        name="dequant",
    )(scale, pltpu.with_memory_space_constraint(weight, pltpu.HBM))


def product(rows, w_ref, store, width=256):
    for j in range(w_ref.shape[1] // width):
        at = slice(j * width, (j + 1) * width)
        store(at, jnp.dot(rows, w_ref[:, at], preferred_element_type=F32).astype(BF16))


def encode_kernel(where_ref, *refs, pieces, chunk):
    w_ref, outs, all_ref = refs[pieces], refs[pieces + 1 : pieces + 1 + Y], refs[-1]
    height = outs[0].shape[0]
    count = height * Y // pieces
    y = where_ref[0]
    rows = jnp.concatenate([ref[chunk * count : (chunk + 1) * count, :] for ref in refs[:pieces]], axis=0)

    def store(at, tile):
        all_ref[:, at] = tile

    product(rows, w_ref, store)
    for p, out in enumerate(outs):
        quarter = lax.rem(y + ORDER[p], Y)
        out[...] = all_ref[pl.ds(pl.multiple_of(quarter * height, height), height), :]


def encode(where, pieces, weight, chunk, chunks):
    depth, width = weight.shape
    rows = sum(piece.shape[0] for piece in pieces) // chunks
    return pl.pallas_call(
        functools.partial(encode_kernel, pieces=len(pieces), chunk=chunk),
        in_specs=[IN_SMEM] + [IN_VMEM] * (len(pieces) + 1),
        out_specs=[IN_VMEM] * Y,
        out_shape=[shape(rows // Y, width)] * Y,
        scratch_shapes=[pltpu.VMEM((rows, width), BF16)],
        compiler_params=params(16),
        cost_estimate=cost(2 * rows * depth * width, 2 * depth * width),
        name="encode",
    )(where, *pieces, weight)


def decode_kernel(where_ref, *refs):
    quarters, w_ref, mine_ref, theirs_ref, all_ref = refs[:Y], refs[Y], refs[Y + 1], refs[Y + 2], refs[Y + 3]
    height, half = quarters[0].shape[0], mine_ref.shape[0]
    y = where_ref[0]
    for p, ref in enumerate(quarters):
        quarter = lax.rem(y + ORDER[p], Y)
        all_ref[pl.ds(pl.multiple_of(quarter * height, height), height), :] = ref[...]

    def store(at, tile):
        mine_ref[:, at] = tile[:half]
        theirs_ref[:, at] = tile[half:]

    product(all_ref[...], w_ref, store)


def decode(where, quarters, weight):
    depth, width = weight.shape
    rows = quarters[0].shape[0] * Y
    return pl.pallas_call(
        decode_kernel,
        in_specs=[IN_SMEM] + [IN_VMEM] * (Y + 1),
        out_specs=[IN_VMEM] * 2,
        out_shape=[shape(rows // 2, width)] * 2,
        scratch_shapes=[pltpu.VMEM((rows, depth), BF16)],
        compiler_params=params(16),
        cost_estimate=cost(2 * rows * depth * width, 2 * depth * width),
        name="decode",
    )(where, *quarters, weight)


def join_kernel(*refs):
    height = refs[0].shape[0]
    for k, ref in enumerate(refs[:-1]):
        refs[-1][k * height : (k + 1) * height, :] = ref[...]


def sum_kernel(*refs, terms):
    ins, outs = refs[:terms], refs[terms:]
    height = outs[0].shape[0]
    for k, out in enumerate(outs):
        at = slice(k * height, (k + 1) * height)
        total = ins[0][at, :].astype(F32)
        for ref in ins[1:]:
            total = total + ref[at, :].astype(F32)
        out[...] = total.astype(BF16)


def added(arrays, cuts, name):
    rows, width = arrays[0].shape
    return whole(
        functools.partial(sum_kernel, terms=len(arrays)), arrays, [shape(rows // cuts, width)] * cuts, name
    )


def activate_kernel(a_ref, b_ref, bias_ref, out_ref):
    preact = (a_ref[...].astype(F32) + b_ref[...].astype(F32)) + bias_ref[...].reshape(1, -1)
    out_ref[...] = jnp.maximum(preact, 0.0).astype(BF16)


def finish_kernel(*refs):
    total = refs[-2][...]
    for ref in refs[:-2]:
        total = total + ref[...].astype(F32)
    refs[-1][...] = total.astype(BF16)


def place_kernel(where_ref, *refs):
    latents, out_ref, sem = refs[:-2], refs[-2], refs[-1]
    y, x, zh, c = (where_ref[i] for i in range(4))
    height = 16
    blocks = latents[0].shape[0] // height
    copies = []
    for a, ref in enumerate(latents):
        n, quarter = a // Y, lax.rem(y + ORDER[a % Y], Y)
        for j in range(blocks):
            b = quarter * blocks + j
            kc, p, k = b // (2 * X), lax.rem(b // 2, X), lax.rem(b, 2)
            kx = jnp.where(p == 1, ORDER[1], jnp.where(p == 2, ORDER[2], p))
            owner = (lax.rem(x + kx, X) * ZH + lax.rem(zh + 2 * (1 - n) + k, ZH)) * C + lax.rem(c + kc, C)
            copies.append(
                pltpu.make_async_copy(
                    ref.at[pl.ds(j * height, height), :],
                    out_ref.at[pl.ds(pl.multiple_of(owner * height, height), height), :],
                    sem.at[a * blocks + j],
                )
            )
    for copy in copies:
        copy.start()
    for copy in copies:
        copy.wait()


def place(where, latents):
    rows, width = latents[0].shape
    rows *= len(latents)
    return pl.pallas_call(
        place_kernel,
        in_specs=[IN_SMEM] + [ANYWHERE] * len(latents),
        out_specs=ANYWHERE,
        out_shape=shape(rows, width),
        scratch_shapes=[pltpu.SemaphoreType.DMA((rows // 16,))],
        compiler_params=params(4),
        cost_estimate=cost(0, 4 * rows * width),
        name="place",
    )(where, *latents)


def after(array, *others):
    return lax.optimization_barrier((array,) + others)[0]


def send(array, axis, size, by):
    return lax.ppermute(array, axis, [(i, (i + by) % size) for i in range(size)])


def fetch_around(array, axis, size):
    return [array] + [send(array, axis, size, -k) for k in ORDER[1:]]


def hand_around(arrays, axis, size):
    return [arrays[0]] + [send(arrays[p], axis, size, ORDER[p]) for p in SENT]


def on_device(acts, enc_weight, enc_scale, enc_bias, dec_weight, dec_scale, dec_bias):
    depth, width = enc_weight.shape[1:]
    own = acts[0]
    rows = own.shape[0]
    chunk = 2 * rows
    where = jnp.stack([lax.axis_index(a) for a in ("y", "x", "zh", "c")]).astype(jnp.int32)
    near, far, back = (send(own, "zh", ZH, -k) for k in (1, 2, 3))
    enc_full = dequant(enc_weight[0], after(jnp.transpose(enc_scale, (2, 0, 1)), where), 2 * BLOCK, False)
    column = whole(join_kernel, [far, back, own, after(near, enc_full)], [shape(ZH * rows, depth)], "join")[0]
    dec_full = dequant(dec_weight[0], after(jnp.transpose(dec_scale, (1, 0, 2)), column), BLOCK, True)
    mine = fetch_around(column, "x", X)
    theirs = [send(piece, "c", C, 1) for piece in mine[:1] + [after(piece, dec_full) for piece in mine[1:]]]
    pieces = mine + theirs
    quarters, own_piece = [], pieces[0]
    for n in range(2):
        terms = list(encode(where, [own_piece] + pieces[1:], enc_full, n, 2))
        own_piece = after(own_piece, terms[0])
        got = hand_around(terms, "y", Y)
        part = added(got, 1, "gather")[0]
        other = send(part, "zl", ZL, 1)
        if False and n == 1:
            other = after(other, quarters[0][1])
        latents = whole(activate_kernel, [part, other, enc_bias], [shape(*part.shape)], "activate")[0]
        quarters.append(fetch_around(latents, "y", Y))
    parts, decoded, got = [], None, None
    for n in range(2):
        own_part = quarters[n][0] if n == 0 else after(quarters[n][0], decoded)
        decoded, theirs = decode(where, [own_part] + quarters[n][1:], dec_full)
        theirs = send(theirs, "c", C, 1)
        if True and n == 1:
            theirs = after(theirs, got[1])
        cuts = added([decoded, theirs], X, "add")
        got = hand_around(cuts, "x", X)
        if False and n == 1:
            got[0] = after(got[0], parts[1])
        low, high = added(got, 2, "fold")
        parts += [send(low, "zh", ZH, 2), send(high, "zh", ZH, 3)] if n == 0 else [low, send(high, "zh", ZH, 1)]
    recon = whole(finish_kernel, parts + [dec_bias], [shape(rows, depth)], "finish")[0]
    return (recon[None], place(where, quarters[0] + quarters[1]))


def solution(mesh):
    axes = ("y", "zl", "x", "zh", "c")
    fine = Mesh(mesh.devices.reshape(Y, ZL, X, ZH, C), axes)
    in_specs = (
        P(LAYER, LAT, None),
        P(LAYER, None, LAT),
        P(LAYER, None, LAT),
        P(LAT),
        P(LAYER, LAT, None),
        P(LAYER, LAT, None),
        P(LAYER, None),
    )
    out_specs = (P(LAYER, LAT, None), P(None, LAT))
    return jax.shard_map(on_device, mesh=fine, in_specs=in_specs, out_specs=out_specs, check_vma=False)
```

```python
import functools

import jax
import jax.numpy as jnp
from jax import lax
from jax.experimental import pallas as pl
from jax.experimental.pallas import tpu as pltpu
from jax.sharding import Mesh, PartitionSpec as P

BLOCK = 128
Y, ZL, X, ZH, C = 4, 2, 4, 4, 2
LAYER, LAT = ("y", "zl"), ("x", "zh", "c")
ORDER = (0, 1, 3, 2)
SENT = (1, 2, 3)
F32, BF16 = jnp.float32, jnp.bfloat16
MIB = 1 << 20
IN_VMEM = pl.BlockSpec(memory_space=pltpu.VMEM)
IN_SMEM = pl.BlockSpec(memory_space=pltpu.SMEM)
ANYWHERE = pl.BlockSpec(memory_space=pl.ANY)


def params(mib):
    return pltpu.CompilerParams(vmem_limit_bytes=mib * MIB)


def cost(flops, moved):
    return pl.CostEstimate(flops=flops, bytes_accessed=moved, transcendentals=0)


def shape(*dims):
    return jax.ShapeDtypeStruct(dims, BF16)


def whole(kernel, ins, outs, name, flops=0, mib=16, where=None):
    moved = sum(a.size * a.dtype.itemsize for a in list(ins) + list(outs))
    place = [] if where is None else [where]
    return pl.pallas_call(
        kernel,
        in_specs=[IN_SMEM] * len(place) + [IN_VMEM] * len(ins),
        out_specs=[IN_VMEM] * len(outs),
        out_shape=list(outs),
        compiler_params=params(mib),
        cost_estimate=cost(flops, moved),
        name=name,
    )(*place, *ins)


def dequant_kernel(scale_ref, w_ref, out_ref, raw_ref, sem, *, by_row):
    rows, width = out_ref.shape
    step, steps = pl.program_id(0), raw_ref.shape[0] // rows

    def read(step):
        at = pl.ds(pl.multiple_of(step * rows, rows), rows)
        return pltpu.make_async_copy(w_ref.at[at, :], raw_ref.at[at, :], sem.at[step])

    @pl.when(step == 0)
    def _():
        for k in range(steps):
            read(k).start()

    read(step).wait()
    for i in range(rows // BLOCK):
        at = pl.ds(pl.multiple_of(step * rows + i * BLOCK, BLOCK), BLOCK)
        for j in range(width // BLOCK):
            columns = slice(j * BLOCK, (j + 1) * BLOCK)
            k = step * (rows // BLOCK) + i
            scale = scale_ref[k, 0, j] if by_row else scale_ref[j, 0, k]
            out_ref[i * BLOCK : (i + 1) * BLOCK, columns] = (raw_ref[at, columns].astype(F32) * scale).astype(BF16)


def dequant(weight, scale, rows, by_row):
    depth, width = weight.shape
    return pl.pallas_call(
        functools.partial(dequant_kernel, by_row=by_row),
        grid=(depth // rows,),
        in_specs=[IN_SMEM, ANYWHERE],
        out_specs=pl.BlockSpec((rows, width), lambda i: (i, 0)),
        out_shape=shape(depth, width),
        scratch_shapes=[pltpu.VMEM((depth, width), BF16), pltpu.SemaphoreType.DMA((depth // rows,))],
        compiler_params=params(16),
        cost_estimate=cost(depth * width, 4 * depth * width),
        name="dequant",
    )(scale, pltpu.with_memory_space_constraint(weight, pltpu.HBM))


def product(rows, w_ref, store, width=256):
    for j in range(w_ref.shape[1] // width):
        at = slice(j * width, (j + 1) * width)
        store(at, jnp.dot(rows, w_ref[:, at], preferred_element_type=F32).astype(BF16))


def encode_kernel(where_ref, *refs, pieces, chunk):
    w_ref, outs, all_ref = refs[pieces], refs[pieces + 1 : pieces + 1 + Y], refs[-1]
    height = outs[0].shape[0]
    count = height * Y // pieces
    y = where_ref[0]
    rows = jnp.concatenate([ref[chunk * count : (chunk + 1) * count, :] for ref in refs[:pieces]], axis=0)

    def store(at, tile):
        all_ref[:, at] = tile

    product(rows, w_ref, store)
    for p, out in enumerate(outs):
        quarter = lax.rem(y + ORDER[p], Y)
        out[...] = all_ref[pl.ds(pl.multiple_of(quarter * height, height), height), :]


def encode(where, pieces, weight, chunk, chunks):
    depth, width = weight.shape
    rows = sum(piece.shape[0] for piece in pieces) // chunks
    return pl.pallas_call(
        functools.partial(encode_kernel, pieces=len(pieces), chunk=chunk),
        in_specs=[IN_SMEM] + [IN_VMEM] * (len(pieces) + 1),
        out_specs=[IN_VMEM] * Y,
        out_shape=[shape(rows // Y, width)] * Y,
        scratch_shapes=[pltpu.VMEM((rows, width), BF16)],
        compiler_params=params(16),
        cost_estimate=cost(2 * rows * depth * width, 2 * depth * width),
        name="encode",
    )(where, *pieces, weight)


def decode_kernel(where_ref, *refs):
    quarters, w_ref, mine_ref, theirs_ref, all_ref = refs[:Y], refs[Y], refs[Y + 1], refs[Y + 2], refs[Y + 3]
    height, half = quarters[0].shape[0], mine_ref.shape[0]
    y = where_ref[0]
    for p, ref in enumerate(quarters):
        quarter = lax.rem(y + ORDER[p], Y)
        all_ref[pl.ds(pl.multiple_of(quarter * height, height), height), :] = ref[...]

    def store(at, tile):
        mine_ref[:, at] = tile[:half]
        theirs_ref[:, at] = tile[half:]

    product(all_ref[...], w_ref, store)


def decode(where, quarters, weight):
    depth, width = weight.shape
    rows = quarters[0].shape[0] * Y
    return pl.pallas_call(
        decode_kernel,
        in_specs=[IN_SMEM] + [IN_VMEM] * (Y + 1),
        out_specs=[IN_VMEM] * 2,
        out_shape=[shape(rows // 2, width)] * 2,
        scratch_shapes=[pltpu.VMEM((rows, depth), BF16)],
        compiler_params=params(16),
        cost_estimate=cost(2 * rows * depth * width, 2 * depth * width),
        name="decode",
    )(where, *quarters, weight)


def join_kernel(*refs):
    height = refs[0].shape[0]
    for k, ref in enumerate(refs[:-1]):
        refs[-1][k * height : (k + 1) * height, :] = ref[...]


def sum_kernel(*refs, terms):
    ins, outs = refs[:terms], refs[terms:]
    height = outs[0].shape[0]
    for k, out in enumerate(outs):
        at = slice(k * height, (k + 1) * height)
        total = ins[0][at, :].astype(F32)
        for ref in ins[1:]:
            total = total + ref[at, :].astype(F32)
        out[...] = total.astype(BF16)


def added(arrays, cuts, name):
    rows, width = arrays[0].shape
    return whole(
        functools.partial(sum_kernel, terms=len(arrays)), arrays, [shape(rows // cuts, width)] * cuts, name
    )


def activate_kernel(a_ref, b_ref, bias_ref, out_ref):
    preact = (a_ref[...].astype(F32) + b_ref[...].astype(F32)) + bias_ref[...].reshape(1, -1)
    out_ref[...] = jnp.maximum(preact, 0.0).astype(BF16)


def finish_kernel(*refs):
    total = refs[-2][...]
    for ref in refs[:-2]:
        total = total + ref[...].astype(F32)
    refs[-1][...] = total.astype(BF16)


def place_kernel(where_ref, *refs):
    latents, out_ref, sem = refs[:-2], refs[-2], refs[-1]
    y, x, zh, c = (where_ref[i] for i in range(4))
    height = 16
    blocks = latents[0].shape[0] // height
    copies = []
    for a, ref in enumerate(latents):
        n, quarter = a // Y, lax.rem(y + ORDER[a % Y], Y)
        for j in range(blocks):
            b = quarter * blocks + j
            kc, p, k = b // (2 * X), lax.rem(b // 2, X), lax.rem(b, 2)
            kx = jnp.where(p == 1, ORDER[1], jnp.where(p == 2, ORDER[2], jnp.where(p == 3, ORDER[3], 0)))
            owner = (lax.rem(x + kx, X) * ZH + lax.rem(zh + 2 * (1 - n) + k, ZH)) * C + lax.rem(c + kc, C)
            copies.append(
                pltpu.make_async_copy(
                    ref.at[pl.ds(j * height, height), :],
                    out_ref.at[pl.ds(pl.multiple_of(owner * height, height), height), :],
                    sem.at[a * blocks + j],
                )
            )
    for copy in copies:
        copy.start()
    for copy in copies:
        copy.wait()


def place(where, latents):
    rows, width = latents[0].shape
    rows *= len(latents)
    return pl.pallas_call(
        place_kernel,
        in_specs=[IN_SMEM] + [ANYWHERE] * len(latents),
        out_specs=ANYWHERE,
        out_shape=shape(rows, width),
        scratch_shapes=[pltpu.SemaphoreType.DMA((rows // 16,))],
        compiler_params=params(4),
        cost_estimate=cost(0, 4 * rows * width),
        name="place",
    )(where, *latents)


def after(array, *others):
    return lax.optimization_barrier((array,) + others)[0]


def send(array, axis, size, by):
    return lax.ppermute(array, axis, [(i, (i + by) % size) for i in range(size)])


def fetch_around(array, axis, size):
    return [array] + [send(array, axis, size, -k) for k in ORDER[1:]]


def hand_around(arrays, axis, size):
    return [arrays[0]] + [send(arrays[p], axis, size, ORDER[p]) for p in SENT]


def on_device(acts, enc_weight, enc_scale, enc_bias, dec_weight, dec_scale, dec_bias):
    depth, width = enc_weight.shape[1:]
    own = acts[0]
    rows = own.shape[0]
    chunk = 2 * rows
    where = jnp.stack([lax.axis_index(a) for a in ("y", "x", "zh", "c")]).astype(jnp.int32)
    near, far, back = (send(own, "zh", ZH, -k) for k in (1, 2, 3))
    enc_full = dequant(enc_weight[0], after(jnp.transpose(enc_scale, (2, 0, 1)), where), 2 * BLOCK, False)
    column = whole(join_kernel, [far, back, own, after(near, enc_full)], [shape(ZH * rows, depth)], "join")[0]
    dec_full = dequant(dec_weight[0], after(jnp.transpose(dec_scale, (1, 0, 2)), column), BLOCK, True)
    mine = fetch_around(column, "x", X)
    theirs = [send(piece, "c", C, 1) for piece in mine[:1] + [after(piece, dec_full) for piece in mine[1:]]]
    pieces = mine + theirs
    quarters, own_piece = [], pieces[0]
    for n in range(2):
        terms = list(encode(where, [own_piece] + pieces[1:], enc_full, n, 2))
        own_piece = after(own_piece, terms[0])
        got = hand_around(terms, "y", Y)
        part = added(got, 1, "gather")[0]
        other = send(part, "zl", ZL, 1)
        if False and n == 1:
            other = after(other, quarters[0][1])
        latents = whole(activate_kernel, [part, other, enc_bias], [shape(*part.shape)], "activate")[0]
        quarters.append(fetch_around(latents, "y", Y))
    parts, decoded, got = [], None, None
    for n in range(2):
        own_part = quarters[n][0] if n == 0 else after(quarters[n][0], decoded)
        decoded, theirs = decode(where, [own_part] + quarters[n][1:], dec_full)
        theirs = send(theirs, "c", C, 1)
        if True and n == 1:
            theirs = after(theirs, got[1])
        cuts = added([decoded, theirs], X, "add")
        got = hand_around(cuts, "x", X)
        if False and n == 1:
            got[0] = after(got[0], parts[1])
        low, high = added(got, 2, "fold")
        parts += [send(low, "zh", ZH, 2), send(high, "zh", ZH, 3)] if n == 0 else [low, send(high, "zh", ZH, 1)]
    recon = whole(finish_kernel, parts + [dec_bias], [shape(rows, depth)], "finish")[0]
    return (recon[None], place(where, quarters[0] + quarters[1]))


def solution(mesh):
    axes = ("y", "zl", "x", "zh", "c")
    fine = Mesh(mesh.devices.reshape(Y, ZL, X, ZH, C), axes)
    in_specs = (
        P(LAYER, LAT, None),
        P(LAYER, None, LAT),
        P(LAYER, None, LAT),
        P(LAT),
        P(LAYER, LAT, None),
        P(LAYER, LAT, None),
        P(LAYER, None),
    )
    out_specs = (P(LAYER, LAT, None), P(None, LAT))
    return jax.shard_map(on_device, mesh=fine, in_specs=in_specs, out_specs=out_specs, check_vma=False)
```
